32 devices in a mesh: fsdp: 2 (over x), ctx: 4 (over y, core), tp: 4 (over z).
Axes of the slice: x: 2, y: 2, z: 4, core: 2. Of those that a mesh axis runs over, the one named last changes fastest.
Arguments:
- tokens: bfloat16 [8, 1024, 1024], P(('fsdp', 'tp'), 'ctx'), may hold values from -6 to 6
- cotangent: bfloat16 [8, 1024, 1024], P(('fsdp', 'tp'), 'ctx'), may hold values from -6 to 6
- mixer_gain: bfloat16 [1024], P(('fsdp', 'ctx', 'tp')), may hold values from 0.5 to 1.5
- mixer_input_weight: bfloat16 [1024, 3328], P(('fsdp', 'ctx', 'tp')), may hold values from -0.1875 to 0.1875
- step_weight: bfloat16 [1024, 24], P(('fsdp', 'ctx', 'tp')), may hold values from -0.1875 to 0.1875
- query_key_value_weight: bfloat16 [1024, 768], P(('fsdp', 'ctx', 'tp')), may hold values from -0.1875 to 0.1875
- conv_weight: bfloat16 [1792, 4], replicated, may hold values from -0.5 to 0.5
- conv_bias: bfloat16 [1792], replicated, may hold values from -0.5 to 0.5
- a_log: bfloat16 [24], replicated, may hold values from 0 to 2.765625
- step_bias: bfloat16 [24], replicated, may hold values from -6.875 to -2.296875
- skip_gain: bfloat16 [24], replicated, may hold values from 0.5 to 1.5
- mixer_output_weight: bfloat16 [1536, 1024], P(('fsdp', 'ctx', 'tp')), may hold values from -0.15625 to 0.15625
- attention_output_weight: bfloat16 [512, 1024], P(('fsdp', 'ctx', 'tp')), may hold values from -4 to 4
- mlp_gain: bfloat16 [1024], P(('fsdp', 'ctx', 'tp')), may hold values from 0.5 to 1.5
- gate_up_weight: bfloat16 [1024, 2, 2048], P(('fsdp', 'ctx'), None, 'tp'), may hold values from -0.1875 to 0.1875
- down_weight: bfloat16 [1024, 2048], P(('fsdp', 'ctx'), 'tp'), may hold values from -0.125 to 0.125
Outputs:
- out_block: bfloat16 [8, 1024, 1024], P(('fsdp', 'tp'), 'ctx')
- grad_tokens: bfloat16 [8, 1024, 1024], P(('fsdp', 'tp'), 'ctx')
- grad_mixer_gain: float32 [1024], P(('fsdp', 'ctx', 'tp'))
- grad_w_zx: float32 [1024, 3328], P(('fsdp', 'ctx', 'tp'))
- grad_w_step: float32 [1024, 24], P(('fsdp', 'ctx', 'tp'))
- grad_w_qkv: float32 [1024, 768], P(('fsdp', 'ctx', 'tp'))
- grad_conv_weight: float32 [1792, 4], replicated
- grad_conv_bias: float32 [1792], replicated
- grad_a_log: float32 [24], replicated
- grad_step_bias: float32 [24], replicated
- grad_skip_gain: float32 [24], replicated
- grad_w_mamba_out: float32 [1536, 1024], P(('fsdp', 'ctx', 'tp'))
- grad_w_attn_out: float32 [512, 1024], P(('fsdp', 'ctx', 'tp'))
- grad_mlp_gain: float32 [1024], P(('fsdp', 'ctx', 'tp'))
- grad_w_gate_up: float32 [1024, 2, 2048], P(('fsdp', 'ctx'), None, 'tp')
- grad_w_down: float32 [1024, 2048], P(('fsdp', 'ctx'), 'tp')
The draws below stay inside these ranges and needn't reach their ends.
All inputs are finite; a program needn't handle non-finite values.
Results may differ from the reference program's by a relative error of at most 0.015.
The reference program's roundings to bfloat16 on the way count: a program that leaves them out, or rounds other values in their place, can miss the bound.
Values may be sent and summed in bfloat16 or wider, within the bound.
A program may use at most 192 MiB of HBM per device.

```python
import jax
import jax.numpy as jnp
from jax import lax

D = 1024
MH = 24
HD = 64
NS = 128
QH = 8
KVH = 2
FF = 2048
CONV_K = 4
SEQ_LEN = 1024
SSD_BLK = 128
SEQS = 8
CONV_CH = 1792


def level_of(stream_key, dims, split, smallest, largest):
    def one(dim, shards_of):
        heights = jax.random.uniform(jax.random.fold_in(jax.random.fold_in(stream_key, 6), dim), (shards_of,), jnp.float32, smallest / len(split), largest / len(split))
        return jnp.repeat(jnp.exp(heights), dims[dim] // shards_of).reshape((-1,) + (1,) * (len(dims) - dim - 1))

    gain = one(*split[0])
    for cut in split[1:]:
        gain = gain * one(*cut)
    return gain


def bell_draw(rng, shape, scale, reach, shards=(), kind=jnp.bfloat16):
    result = jax.random.normal(rng, shape, jnp.float32) * scale
    if len(shards) > 0:
        result = level_of(rng, shape, shards, -0.22, 0.18) * result
    return jnp.clip(result, min=-reach, max=reach).astype(kind)


def setup_inputs(seed: int = 0) -> dict:
    keys = jax.random.split(jax.random.key(seed), 17)
    tokens = bell_draw(keys[0], (SEQS, SEQ_LEN, D), 1.0, 6.0, ((0, 8), (1, 4)))
    cotangent = bell_draw(keys[1], (SEQS, SEQ_LEN, D), 1.0, 6.0, ((0, 8), (1, 4)))
    mixer_gain = jnp.clip(1.0 + 0.1 * jax.random.normal(keys[2], (D,), jnp.float32), 0.5, 1.5).astype(jnp.bfloat16)
    mixer_input_weight = bell_draw(keys[3], (D, 2 * MH * HD + 2 * NS), D ** -0.5, 0.1875, ((0, 32),))
    step_weight = bell_draw(keys[4], (D, MH), D ** -0.5, 0.1875, ((0, 32),))
    query_key_value_weight = bell_draw(keys[5], (D, (QH + 2 * KVH) * HD), D ** -0.5, 0.1875, ((0, 32),))
    conv_weight = jnp.clip(jax.random.uniform(keys[6], (CONV_CH, CONV_K), jnp.float32, -0.5, 0.5), -0.5, 0.5).astype(jnp.bfloat16)
    conv_bias = jnp.clip(jax.random.uniform(keys[7], (CONV_CH,), jnp.float32, -0.5, 0.5), -0.5, 0.5).astype(jnp.bfloat16)
    a_log = jnp.clip(jax.random.uniform(keys[8], (MH,), jnp.float32, 0.0, 2.765625), 0.0, 2.765625).astype(jnp.bfloat16)
    step_bias = jnp.clip(jax.random.uniform(keys[9], (MH,), jnp.float32, -6.875, -2.296875), -6.875, -2.296875).astype(jnp.bfloat16)
    skip_gain = jnp.clip(jax.random.uniform(keys[10], (MH,), jnp.float32, 0.5, 1.5), 0.5, 1.5).astype(jnp.bfloat16)
    mixer_output_weight = bell_draw(keys[11], (MH * HD, D), (MH * HD) ** -0.5, 0.15625, ((0, 32),))
    attention_output_weight = bell_draw(keys[12], (QH * HD, D), (max(QH * HD // 256, 1)) ** -0.5, 4.0, ((0, 32),))
    mlp_gain = jnp.clip(1.0 + 0.1 * jax.random.normal(keys[13], (D,), jnp.float32), 0.5, 1.5).astype(jnp.bfloat16)
    gate_up_weight = bell_draw(keys[14], (D, 2, FF), D ** -0.5, 0.1875, ((0, 8), (2, 4)))
    down_weight = bell_draw(keys[15], (D, FF), FF ** -0.5, 0.125, ((0, 8), (1, 4)))
    return {"tokens": tokens, "cotangent": cotangent, "mixer_gain": mixer_gain, "mixer_input_weight": mixer_input_weight, "step_weight": step_weight, "query_key_value_weight": query_key_value_weight, "conv_weight": conv_weight, "conv_bias": conv_bias, "a_log": a_log, "step_bias": step_bias, "skip_gain": skip_gain, "mixer_output_weight": mixer_output_weight, "attention_output_weight": attention_output_weight, "mlp_gain": mlp_gain, "gate_up_weight": gate_up_weight, "down_weight": down_weight}


@jax.custom_vjp
def low(v):
    return lax.optimization_barrier(v.astype(jnp.bfloat16)).astype(jnp.float32)

@jax.custom_vjp
def reduced_backward(v):
    return v

def low_keep(v):
    return (low(v), None)

def low_pass(kept, grad):
    return (grad,)

def back_keep(v):
    return (v, None)

def back_low(kept, grad):
    return (low(grad),)
low.defvjp(low_keep, low_pass)
reduced_backward.defvjp(back_keep, back_low)

def matrix_product(form, left, right):
    return jnp.einsum(form, left, right, precision=lax.Precision.HIGHEST)

def rms_scale(values_in):
    return lax.rsqrt(lax.optimization_barrier(jnp.mean(values_in * values_in, axis=-1, keepdims=True)) + 1e-05)

def rotate(vectors, positions):
    half_dim = HD // 2
    frequency = 10000.0 ** (-(jnp.arange(half_dim).astype(jnp.float32) * 2.0 / HD))
    angles = positions.astype(jnp.float32)[:, None] * frequency[None, :]
    cosine = jnp.cos(angles)[:, None, :]
    sine_part = jnp.sin(angles)[:, None, :]
    first_half = vectors[..., :half_dim]
    second = vectors[..., half_dim:]
    return jnp.concatenate([first_half * cosine - second * sine_part, second * cosine + first_half * sine_part], axis=-1)

def state_scan(input_values, input_matrix_projection, output_matrix_projection, step_length, rate_neg):
    length, head_count, _ = input_values.shape
    blocks = length // SSD_BLK
    logarithmic_decay = step_length * rate_neg[None, :]
    triangle = jnp.arange(SSD_BLK)[:, None] >= jnp.arange(SSD_BLK)[None, :]

    def regroup_blocks(input_array):
        return input_array.reshape((blocks, SSD_BLK) + input_array.shape[1:])

    def move_forward(states, block_in):
        x_blk, b_blk, c_blk, step_blk, log_blk = block_in
        cumulative = jnp.cumsum(log_blk, axis=0)
        inner_cb = matrix_product('tn,sn->ts', c_blk, b_blk)
        spread = cumulative[:, None, :] - cumulative[None, :, :]
        mixing = inner_cb[:, :, None] * jnp.exp(jnp.where(triangle[:, :, None], spread, -jnp.inf)) * step_blk[None, :, :]
        inside = matrix_product('tsh,shp->thp', mixing, x_blk)
        carried = matrix_product('tn,hpn->thp', c_blk, states) * jnp.exp(cumulative)[:, :, None]
        last_sum = cumulative[-1]
        fading = jnp.exp(last_sum[None, :] - cumulative) * step_blk
        renewed = jnp.exp(last_sum)[:, None, None] * states + matrix_product('shp,sn->hpn', fading[:, :, None] * x_blk, b_blk)
        return (renewed, inside + carried)
    initial_state = jnp.zeros((head_count, HD, NS), input_values.dtype)
    final_state, output_values = lax.scan(move_forward, initial_state, (regroup_blocks(input_values), regroup_blocks(input_matrix_projection), regroup_blocks(output_matrix_projection), regroup_blocks(step_length), regroup_blocks(logarithmic_decay)))
    return output_values.reshape(length, head_count, HD)

def mamba_seq(pre_conv, step_raw, conv_w, conv_b, log_rate, step_shift, skip_scale):
    length = pre_conv.shape[0]
    taps = conv_w.shape[1]
    padded = jnp.pad(pre_conv, ((taps - 1, 0), (0, 0)))
    conv_sum = jnp.broadcast_to(conv_b[None, :], pre_conv.shape)
    for offset in range(taps):
        conv_sum = conv_sum + padded[offset:offset + length] * conv_w[None, :, offset]
    activated = jax.nn.silu(conv_sum)
    head_count = step_raw.shape[1]
    input_values = activated[:, :head_count * HD].reshape(length, head_count, HD)
    input_matrix_projection = activated[:, head_count * HD:head_count * HD + NS]
    output_matrix_projection = activated[:, head_count * HD + NS:]
    step_length = jax.nn.softplus(step_raw + step_shift[None, :])
    output_values = state_scan(input_values, input_matrix_projection, output_matrix_projection, step_length, -jnp.exp(log_rate))
    return (output_values + skip_scale[None, :, None] * input_values).reshape(length, head_count * HD)

def attention_seq(queries, key_heads, value_heads):
    length = queries.shape[0]
    positions = jnp.arange(length)
    query_rot = low(rotate(queries, positions))
    key_rot = low(rotate(key_heads, positions))
    key_rep = jnp.repeat(key_rot, QH // KVH, axis=1)
    value_rep = jnp.repeat(value_heads, QH // KVH, axis=1)
    scores = reduced_backward(matrix_product('qhd,khd->hqk', query_rot, key_rep) * HD ** (-0.5))
    causal = positions[None, :] <= positions[:, None]
    scores = jnp.where(causal[None], scores, -jnp.inf)
    attn_probs = jax.nn.softmax(scores, axis=-1)
    return matrix_product('hqk,khd->qhd', low(attn_probs), value_rep).reshape(length, QH * HD)

def forward(tokens, mixer_gain, mixer_input_weight, step_weight, query_key_value_weight, conv_weight, conv_bias, a_log, step_bias, skip_gain, mixer_output_weight, attention_output_weight, mlp_gain, gate_up_weight, down_weight):
    seq_count, length, _ = tokens.shape
    mamba_width = MH * HD
    first_normalized = low(tokens * rms_scale(tokens) * mixer_gain)
    mixer_input_projection = reduced_backward(matrix_product('tzf,fh->tzh', first_normalized, mixer_input_weight))
    step_projection = reduced_backward(matrix_product('tzf,fh->tzh', first_normalized, step_weight))
    query_key_value_projection = reduced_backward(matrix_product('tzf,fh->tzh', first_normalized, query_key_value_weight))
    gate_z = mixer_input_projection[..., :mamba_width]
    conv_in = low(mixer_input_projection[..., mamba_width:])
    step_raw = low(step_projection)
    qkv_sent = low(query_key_value_projection)
    queries = qkv_sent[..., :QH * HD].reshape(seq_count, length, QH, HD)
    key_heads = qkv_sent[..., QH * HD:(QH + KVH) * HD].reshape(seq_count, length, KVH, HD)
    value_heads = qkv_sent[..., (QH + KVH) * HD:].reshape(seq_count, length, KVH, HD)
    mamba_out = lax.map(jax.checkpoint(lambda operands: mamba_seq(operands[0], operands[1], conv_weight, conv_bias, a_log, step_bias, skip_gain)), (conv_in, step_raw))
    mamba_sent = reduced_backward(low(mamba_out))
    gated_mixture = low(mamba_sent * jax.nn.silu(gate_z))
    attn_out = lax.map(jax.checkpoint(lambda operands: attention_seq(operands[0], operands[1], operands[2])), (queries, key_heads, value_heads))
    attention_dispatched = reduced_backward(low(attn_out))
    branch_output = matrix_product('ajv,vx->ajx', gated_mixture, mixer_output_weight) + matrix_product('ajv,vx->ajx', attention_dispatched, attention_output_weight)
    residual_stream = tokens + reduced_backward(branch_output)
    second_normalized = low(residual_stream * rms_scale(residual_stream) * mlp_gain)
    gate_up_values = reduced_backward(matrix_product('tvx,xiw->tviw', second_normalized, gate_up_weight))
    hidden_units = low(jax.nn.silu(gate_up_values[..., 0, :]) * gate_up_values[..., 1, :])
    return residual_stream + matrix_product('gnh,yh->gny', hidden_units, down_weight)

def reference(tokens, cotangent, mixer_gain, mixer_input_weight, step_weight, query_key_value_weight, conv_weight, conv_bias, a_log, step_bias, skip_gain, mixer_output_weight, attention_output_weight, mlp_gain, gate_up_weight, down_weight):
    primals = [tokens, mixer_gain, mixer_input_weight, step_weight, query_key_value_weight, conv_weight, conv_bias, a_log, step_bias, skip_gain, mixer_output_weight, attention_output_weight, mlp_gain, gate_up_weight, down_weight]
    primals = [input_array.astype(jnp.float32) for input_array in primals]
    out_block, pullback = jax.vjp(forward, *primals)
    grads = pullback(cotangent.astype(jnp.float32))
    return (out_block.astype(jnp.bfloat16), grads[0].astype(jnp.bfloat16), grads[1], grads[2], grads[3], grads[4], grads[5], grads[6], grads[7], grads[8], grads[9], grads[10], grads[11], grads[12], grads[13], grads[14])
```

```python
import jax
import jax.numpy as jnp
from jax import lax
from jax.experimental import pallas as pl
from jax.experimental.pallas import tpu as pltpu
from jax.sharding import PartitionSpec as P

MH = 24
HD = 64
NS = 128
QH = 8
KVH = 2
SSD_BLK = 128
ATT_BLK = 512


def product(form, left, right):
    return jnp.einsum(form, left, right, preferred_element_type=jnp.float32)


def matrix_product(form, left, right):
    return jnp.einsum(form, left, right, precision=lax.Precision.HIGHEST)


def rms_scale(values_in):
    return lax.rsqrt(jnp.mean(values_in * values_in, axis=-1, keepdims=True) + 1e-05)


def norm_back(values_in, scale_in, gain_in, grad_normed):
    weighted = grad_normed * gain_in
    grad_values = scale_in * weighted - values_in * scale_in**3 * jnp.mean(
        weighted * values_in, axis=-1, keepdims=True
    )
    grad_gain = jnp.sum(grad_normed * values_in * scale_in, axis=(0, 1))
    return (grad_values, grad_gain)


def rotate(vectors, positions, direction):
    half_dim = HD // 2
    frequency = 10000.0 ** (-(jnp.arange(half_dim, dtype=jnp.float32) * 2.0 / HD))
    angles = positions.astype(jnp.float32)[:, None] * frequency[None, :]
    cosine = jnp.cos(angles)[:, None, :]
    sine_part = direction * jnp.sin(angles)[:, None, :]
    first_half = vectors[..., :half_dim]
    second = vectors[..., half_dim:]
    return jnp.concatenate(
        [first_half * cosine - second * sine_part, second * cosine + first_half * sine_part],
        axis=-1,
    )


def exact_dot(left, right, left_dim, right_dim):
    return lax.dot_general(
        left,
        right,
        (((left_dim,), (right_dim,)), ((), ())),
        precision=lax.Precision.HIGHEST,
        preferred_element_type=jnp.float32,
    )


def low_half(rows):
    return lax.broadcasted_iota(jnp.int32, (rows, 2 * HD), 1) < HD


def spread_heads(per_head):
    rows, heads = per_head.shape
    lower = low_half(rows)
    return jnp.concatenate(
        [
            jnp.where(lower, per_head[:, h : h + 1], per_head[:, h + 1 : h + 2])
            for h in range(0, heads, 2)
        ],
        axis=1,
    )


def head_sums_of(wide):
    rows, width = wide.shape
    lower = low_half(rows)
    sums = []
    for start in range(0, width, 2 * HD):
        pair = wide[:, start : start + 2 * HD]
        sums.append(jnp.sum(jnp.where(lower, pair, 0.0), axis=1, keepdims=True))
        sums.append(jnp.sum(jnp.where(lower, 0.0, pair), axis=1, keepdims=True))
    return jnp.concatenate(sums, axis=1)


def split_pair(wide, start):
    pair = wide[:, start : start + 2 * HD]
    lower = low_half(pair.shape[0])
    return jnp.concatenate(
        [jnp.where(lower, pair, 0.0), jnp.where(lower, 0.0, pair)], axis=0
    )


def decay_of(cum, cum_row, h):
    blk = cum.shape[0]
    rows = lax.broadcasted_iota(jnp.int32, (blk, blk), 0)
    columns = lax.broadcasted_iota(jnp.int32, (blk, blk), 1)
    spread = cum[:, h : h + 1] - cum_row[h : h + 1, :]
    return jnp.exp(jnp.where(rows >= columns, spread, -1e30))


def scan_forward_kernel(
    x_ref, b_ref, c_ref, step_ref, cum_ref, step_row_ref, cum_row_ref, y_ref, kept_ref, state
):
    @pl.when(pl.program_id(1) == 0)
    def _():
        state[...] = jnp.zeros_like(state)

    x, bmat, cmat = x_ref[0], b_ref[0], c_ref[0]
    step, cum, step_row, cum_row = step_ref[0], cum_ref[0], step_row_ref[0], cum_row_ref[0]
    blk, heads = step.shape
    before = state[...]
    kept_ref[0, 0] = before
    inner = exact_dot(cmat, bmat, 1, 1)
    carried = exact_dot(cmat, before, 1, 0) * spread_heads(jnp.exp(cum))
    for h in range(0, heads, 2):
        mixing = jnp.concatenate(
            [inner * decay_of(cum, cum_row, k) * step_row[k : k + 1, :] for k in (h, h + 1)],
            axis=1,
        )
        columns = slice(h * HD, (h + 2) * HD)
        y_ref[0, :, columns] = (
            exact_dot(mixing, split_pair(x, h * HD), 1, 0) + carried[:, columns]
        )
    last = cum[blk - 1 :, :]
    fading = spread_heads(jnp.exp(last - cum) * step)
    state[...] = spread_heads(jnp.exp(last)) * before + exact_dot(bmat, fading * x, 0, 0)


def scan_backward_kernel(
    x_ref,
    b_ref,
    c_ref,
    step_ref,
    cum_ref,
    step_row_ref,
    cum_row_ref,
    kept_ref,
    up_ref,
    gx_ref,
    gb_ref,
    gc_ref,
    gstep_ref,
    gcum_ref,
    gstep_row_ref,
    gcum_row_ref,
    gstate,
):
    @pl.when(pl.program_id(1) == 0)
    def _():
        gstate[...] = jnp.zeros_like(gstate)

    x, bmat, cmat, up = x_ref[0], b_ref[0], c_ref[0], up_ref[0]
    step, cum, step_row, cum_row = step_ref[0], cum_ref[0], step_row_ref[0], cum_row_ref[0]
    blk, heads = step.shape
    before = kept_ref[0, 0]
    after = gstate[...]
    up_decayed = up * spread_heads(jnp.exp(cum))
    last = cum[blk - 1 :, :]
    weight = jnp.exp(last - cum)
    fading = weight * step
    fading_wide = spread_heads(fading)
    from_state = exact_dot(cmat, before, 1, 0)
    onto_x = exact_dot(bmat, after, 1, 0)
    grad_c = exact_dot(up_decayed, before, 1, 1)
    grad_b = exact_dot(fading_wide * x, after, 1, 1)
    meeting = head_sums_of(x * onto_x)
    gstep_ref[0] = weight * meeting
    leaving = fading * meeting
    end_part = jnp.sum(leaving, axis=0, keepdims=True) + jnp.exp(last) * head_sums_of(
        jnp.sum(after * before, axis=0, keepdims=True)
    )
    is_last = lax.broadcasted_iota(jnp.int32, (blk, heads), 0) == blk - 1
    grad_cum = (
        head_sums_of(up_decayed * from_state) - leaving + jnp.where(is_last, end_part, 0.0)
    )
    gstate[...] = spread_heads(jnp.exp(last)) * after + exact_dot(cmat, up_decayed, 0, 0)
    inner = exact_dot(cmat, bmat, 1, 1)
    grad_inner = jnp.zeros((blk, blk), jnp.float32)
    row_parts = []
    for h in range(0, heads, 2):
        columns = slice(h * HD, (h + 2) * HD)
        up_pair = split_pair(up, h * HD)
        grad_pair = exact_dot(up_pair, x[:, columns], 1, 1)
        mixings = []
        for k in (h, h + 1):
            decay = decay_of(cum, cum_row, k)
            row = step_row[k : k + 1, :]
            decayed = grad_pair[(k - h) * blk : (k - h + 1) * blk] * decay
            grad_inner += decayed * row
            both = decayed * inner
            row_sum = jnp.sum(both, axis=0, keepdims=True)
            gstep_row_ref[0, k : k + 1, :] = row_sum
            gcum_row_ref[0, k : k + 1, :] = -row_sum * row
            row_parts.append(jnp.sum(both * row, axis=1, keepdims=True))
            mixings.append(inner * decay * row)
        gx_ref[0, :, columns] = fading_wide[:, columns] * onto_x[:, columns] + exact_dot(
            jnp.concatenate(mixings, axis=0), up_pair, 0, 0
        )
    gcum_ref[0] = grad_cum + jnp.concatenate(row_parts, axis=1)
    gb_ref[0] = grad_b + exact_dot(grad_inner, cmat, 0, 0)
    gc_ref[0] = grad_c + exact_dot(grad_inner, bmat, 1, 0)


def scan_specs(heads, flip):
    def row_block(width):
        return pl.BlockSpec((1, SSD_BLK, width), lambda s, j: (s, flip(j), 0))

    across = pl.BlockSpec((1, heads, SSD_BLK), lambda s, j: (s, 0, flip(j)))
    kept = pl.BlockSpec((1, 1, NS, heads * HD), lambda s, j: (s, flip(j), 0, 0))
    return row_block, across, kept


def scan_call(body, ins, flip, backward):
    seqs, length, width = ins[0].shape
    heads = width // HD
    blocks = length // SSD_BLK
    row_block, across, kept = scan_specs(heads, flip)
    wide, state, slim = row_block(width), row_block(NS), row_block(heads)
    in_specs = [wide, state, state, slim, slim, across, across]

    def f32(*shape):
        return jax.ShapeDtypeStruct(shape, jnp.float32)

    if backward:
        in_specs = in_specs + [kept, wide]
        out_specs = [wide, state, state, slim, slim, across, across]
        out_shape = [
            f32(seqs, length, width),
            f32(seqs, length, NS),
            f32(seqs, length, NS),
            f32(seqs, length, heads),
            f32(seqs, length, heads),
            f32(seqs, heads, length),
            f32(seqs, heads, length),
        ]
    else:
        out_specs = [wide, kept]
        out_shape = [f32(seqs, length, width), f32(seqs, blocks, NS, width)]
    return pl.pallas_call(
        body,
        grid=(seqs, blocks),
        in_specs=in_specs,
        out_specs=out_specs,
        out_shape=out_shape,
        scratch_shapes=[pltpu.VMEM((NS, width), jnp.float32)],
        compiler_params=pltpu.CompilerParams(
            dimension_semantics=("arbitrary", "arbitrary"), vmem_limit_bytes=32 * 1024 * 1024
        ),
        cost_estimate=pl.CostEstimate(
            flops=20_000_000_000 if backward else 8_000_000_000,
            bytes_accessed=12_000_000,
            transcendentals=2_000_000,
        ),
    )(*ins)


def mamba_prepare(pre_conv, step_raw, conv_w, conv_b, log_rate, step_shift):
    seqs, length, _ = pre_conv.shape
    taps = conv_w.shape[1]
    heads = step_raw.shape[-1]
    padded = jnp.pad(pre_conv, ((0, 0), (taps - 1, 0), (0, 0)))
    conv_sum = conv_b[None, None, :]
    for offset in range(taps):
        conv_sum = conv_sum + padded[:, offset : offset + length] * conv_w[:, offset]
    activated = jax.nn.silu(conv_sum)
    step = jax.nn.softplus(step_raw + step_shift)
    logs = (step * -jnp.exp(log_rate)).reshape(seqs, length // SSD_BLK, SSD_BLK, heads)
    lower = jnp.tril(jnp.ones((SSD_BLK, SSD_BLK), jnp.float32))
    cum = matrix_product("ts,gbsh->gbth", lower, logs).reshape(seqs, length, heads)
    width = heads * HD
    return (
        activated[..., :width],
        activated[..., width : width + NS],
        activated[..., width + NS :],
        step,
        cum,
    )


def masked_scores(query_blk, key_seq, row_start, key_pos):
    scores = product("qhd,khd->hqk", query_blk, key_seq) * HD ** (-0.5)
    query_pos = row_start + jnp.arange(ATT_BLK)
    return jnp.where(key_pos[None, None, :] <= query_pos[None, :, None], scores, -jnp.inf)


def attend_forward(queries, key_rot, values):
    seq_count, length, head_count, _ = queries.shape
    blocks = length // ATT_BLK
    key_pos = jnp.arange(length)

    def one_block(flat_index):
        seq_index = flat_index // blocks
        row_start = flat_index % blocks * ATT_BLK
        query_blk = lax.dynamic_slice(
            queries, (seq_index, row_start, 0, 0), (1, ATT_BLK, head_count, HD)
        )[0]
        key_seq = lax.dynamic_index_in_dim(key_rot, seq_index, 0, keepdims=False)
        value_seq = lax.dynamic_index_in_dim(values, seq_index, 0, keepdims=False)
        scores = masked_scores(query_blk, key_seq, row_start, key_pos)
        row_peak = jnp.max(scores, axis=-1, keepdims=True)
        raised = jnp.exp(scores - row_peak)
        totals = jnp.sum(raised, axis=-1, keepdims=True)
        attn_probs = raised / totals
        output = product("hqk,khd->qhd", attn_probs.astype(jnp.bfloat16), value_seq)
        return (output, row_peak[..., 0] + jnp.log(totals[..., 0]))

    output_values, logsum = lax.map(one_block, jnp.arange(seq_count * blocks))
    return (
        output_values.reshape(seq_count, length, head_count, HD),
        logsum.reshape(seq_count, blocks, head_count, ATT_BLK),
    )


def attend_backward(queries, key_rot, values, logsum, grad_out):
    seq_count, length, head_count, _ = queries.shape
    blocks = length // ATT_BLK
    key_pos = jnp.arange(length)
    score_scale = HD ** (-0.5)

    def attend_one_seq(operands):
        query_seq, key_seq, value_seq, logsum_seq, grad_seq = operands

        def one_move_forward(running, blk_index):
            grad_keys_acc, grad_values_acc = running
            row_start = blk_index * ATT_BLK
            query_blk = lax.dynamic_slice_in_dim(query_seq, row_start, ATT_BLK, 0)
            grad_blk = lax.dynamic_slice_in_dim(grad_seq, row_start, ATT_BLK, 0)
            scores = masked_scores(query_blk, key_seq, row_start, key_pos)
            attn_probs = jnp.exp(
                scores
                - lax.dynamic_index_in_dim(logsum_seq, blk_index, 0, keepdims=False)[:, :, None]
            )
            probs_low = attn_probs.astype(jnp.bfloat16)
            grad_probs = product("qhd,khd->hqk", grad_blk, value_seq)
            offset_mean = jnp.sum(attn_probs * grad_probs, axis=-1, keepdims=True)
            grad_scores = (attn_probs * (grad_probs - offset_mean)).astype(jnp.bfloat16)
            grad_query_blk = product("hqk,khd->qhd", grad_scores, key_seq) * score_scale
            grad_keys_acc = (
                grad_keys_acc + product("hqk,qhd->khd", grad_scores, query_blk) * score_scale
            )
            grad_values_acc = grad_values_acc + product("hqk,qhd->khd", probs_low, grad_blk)
            return ((grad_keys_acc, grad_values_acc), grad_query_blk)

        zeros_kv = jnp.zeros((length, head_count, HD), jnp.float32)
        (grad_keys_seq, grad_values_seq), grad_query_blocks = lax.scan(
            one_move_forward, (zeros_kv, zeros_kv), jnp.arange(blocks)
        )
        return (grad_query_blocks.reshape(length, head_count, HD), grad_keys_seq, grad_values_seq)

    return lax.map(attend_one_seq, (queries, key_rot, values, logsum, grad_out))


def pair_half(parts, axis_name, dim, place, count):
    idx = lax.axis_index(axis_name)
    bit = (idx // place) % 2
    kept = lax.dynamic_index_in_dim(parts, bit, dim, keepdims=False)
    given = lax.dynamic_index_in_dim(parts, 1 - bit, dim, keepdims=False)
    got = lax.ppermute(given, axis_name, [(i, i ^ place) for i in range(count)])
    return kept.astype(jnp.float32) + got.astype(jnp.float32)


def scatter_sum(parts, axes, rows_first=False):
    bits = []
    for name in axes:
        count = lax.axis_size(name)
        place = count // 2
        while place:
            bits.append((name, place, count))
            place //= 2
    shape = parts.shape[1:]
    parts = parts.reshape((2,) * len(bits) + shape)
    near = [bit for bit in bits if bit[0] == "ctx"][::-1]
    rows = [bit for bit in bits if bit[0] == "fsdp"]
    order = near[:1] + rows + near[1:] if rows_first else near + rows
    order = order + [bit for bit in bits if bit[0] == "tp"]
    left = list(bits)
    for bit in order:
        dim = left.index(bit)
        parts = pair_half(parts.astype(jnp.bfloat16), bit[0], dim, bit[1], bit[2])
        left.remove(bit)
    return parts.reshape(shape)


def butterfly_sum(value, axes):
    for name in axes:
        count = lax.axis_size(name)
        place = 1
        while place < count:
            value = value + lax.ppermute(value, name, [(i, i ^ place) for i in range(count)])
            place *= 2
    return value


def line_gather(value, name):
    count = lax.axis_size(name)
    here = lax.axis_index(name)
    up, down = [value], [value]
    for _ in range(count - 1):
        up.append(lax.ppermute(up[-1], name, [(i, i + 1) for i in range(count - 1)]))
        down.append(lax.ppermute(down[-1], name, [(i + 1, i) for i in range(count - 1)]))
    blocks = []
    for owner in range(count):
        block = value
        for away in range(1, count):
            block = jnp.where(here - owner == away, up[away], block)
            block = jnp.where(owner - here == away, down[away], block)
        blocks.append(block)
    return jnp.concatenate(blocks, axis=0)


def on_device(
    tokens,
    cotangent,
    mixer_gain,
    mixer_input_weight,
    step_weight,
    query_key_value_weight,
    conv_weight,
    conv_bias,
    a_log,
    step_bias,
    skip_gain,
    mixer_output_weight,
    attention_output_weight,
    mlp_gain,
    gate_up_weight,
    down_weight,
):
    seq_count, local_len, _ = tokens.shape
    ctx_size = lax.axis_size("ctx")
    ctx_index = lax.axis_index("ctx")
    mamba_width = MH * HD
    heads_dev = MH // ctx_size
    query_dev = QH // ctx_size
    x_dev = heads_dev * HD
    q_dev = query_dev * HD
    full_len = local_len * ctx_size

    devices_axes = ("fsdp", "ctx", "tp")
    zx_cols = mixer_input_weight.shape[1]
    qkv_cols = query_key_value_weight.shape[1]
    packed_cols = -(-(zx_cols + qkv_cols + MH + 2) // 128) * 128
    in_packed = jnp.concatenate(
        [
            mixer_input_weight,
            query_key_value_weight,
            step_weight,
            mixer_gain[:, None],
            mlp_gain[:, None],
            jnp.zeros(
                (mixer_gain.shape[0], packed_cols - zx_cols - qkv_cols - MH - 2), jnp.bfloat16
            ),
        ],
        axis=1,
    )
    in_full = lax.all_gather(in_packed, devices_axes, axis=0, tiled=True)
    zx_full = in_full[:, :zx_cols]
    qkv_full = in_full[:, zx_cols : zx_cols + qkv_cols]
    step_full = in_full[:, zx_cols + qkv_cols : zx_cols + qkv_cols + MH]
    gain_one = in_full[:, zx_cols + qkv_cols + MH]
    gain_two = in_full[:, zx_cols + qkv_cols + MH + 1]
    out_rows = mixer_output_weight.shape[0]
    out_packed = jnp.concatenate([mixer_output_weight, attention_output_weight], axis=0)
    out_full = lax.all_gather(out_packed, devices_axes, axis=0)
    gate_up_full = lax.all_gather(gate_up_weight, ("fsdp", "ctx"), axis=0, tiled=True)
    down_full = lax.all_gather(down_weight, ("fsdp", "ctx"), axis=0, tiled=True)
    cot_all = line_gather(cotangent, "tp")
    tokens_f = tokens.astype(jnp.float32)
    scale_one = rms_scale(tokens_f)
    first_normalized = (tokens_f * scale_one * gain_one.astype(jnp.float32)).astype(jnp.bfloat16)
    mixer_input_projection = product("gld,de->gle", first_normalized, zx_full)
    step_projection = product("gld,de->gle", first_normalized, step_full).astype(jnp.bfloat16)
    query_key_value_projection = product("gld,de->gle", first_normalized, qkv_full).astype(
        jnp.bfloat16
    )
    gate_z = mixer_input_projection[..., :mamba_width]
    conv_in = mixer_input_projection[..., mamba_width:].astype(jnp.bfloat16)
    group = QH // KVH
    kv_dev = max(query_dev // group, 1)
    kv_copies = kv_dev * ctx_size // KVH
    kv_cols = kv_dev * HD
    send_cols = x_dev + q_dev + 2 * NS + 2 * kv_cols
    step_cols = -(send_cols + heads_dev) % 128 + heads_dev

    def to_heads(rows):
        pieces = rows.reshape(seq_count, local_len, ctx_size, -1)
        return jnp.transpose(pieces, (2, 0, 1, 3))

    def to_all(rows):
        return jnp.broadcast_to(rows[None], (ctx_size,) + rows.shape)

    def exchange(pieces):
        return lax.all_to_all(pieces, "ctx", split_axis=0, concat_axis=0, tiled=True)

    def to_sequence(pieces):
        return jnp.transpose(pieces, (1, 0, 2, 3)).reshape(seq_count, full_len, -1)

    def to_parts(rows):
        return jnp.transpose(
            rows.reshape(seq_count, ctx_size, local_len, rows.shape[-1]), (1, 0, 2, 3)
        )

    def join_heads(pieces):
        return jnp.transpose(pieces, (1, 2, 0, 3)).reshape(seq_count, local_len, -1)

    def kv_pieces(rows):
        heads = jnp.repeat(rows.reshape(seq_count, local_len, KVH, HD), kv_copies, axis=2)
        return to_heads(heads)

    heads_send = jnp.concatenate(
        [
            to_heads(conv_in[..., :mamba_width]),
            to_heads(query_key_value_projection[..., : QH * HD]),
            to_all(conv_in[..., mamba_width:]),
            kv_pieces(query_key_value_projection[..., QH * HD : (QH + KVH) * HD]),
            kv_pieces(query_key_value_projection[..., (QH + KVH) * HD :]),
            to_heads(step_projection),
            jnp.zeros(
                (ctx_size, seq_count, local_len, step_cols - heads_dev), jnp.bfloat16
            ),
        ],
        axis=-1,
    )
    heads_send, cot_all = lax.optimization_barrier((heads_send, cot_all))
    heads_in = to_sequence(exchange(heads_send))
    bc_start = x_dev + q_dev
    key_start = bc_start + 2 * NS
    value_start = key_start + kv_cols
    step_heads = heads_in[..., send_cols : send_cols + heads_dev]
    conv_rows = jnp.concatenate(
        [
            lax.dynamic_slice_in_dim(conv_weight, ctx_index * x_dev, x_dev, 0),
            conv_weight[mamba_width:],
        ],
        axis=0,
    ).astype(jnp.float32)
    bias_rows = jnp.concatenate(
        [lax.dynamic_slice_in_dim(conv_bias, ctx_index * x_dev, x_dev, 0), conv_bias[mamba_width:]],
        axis=0,
    ).astype(jnp.float32)
    rate_rows = lax.dynamic_slice_in_dim(a_log, ctx_index * heads_dev, heads_dev, 0).astype(
        jnp.float32
    )
    shift_rows = lax.dynamic_slice_in_dim(step_bias, ctx_index * heads_dev, heads_dev, 0).astype(
        jnp.float32
    )
    skip_rows = lax.dynamic_slice_in_dim(skip_gain, ctx_index * heads_dev, heads_dev, 0).astype(
        jnp.float32
    )
    mamba_in = jnp.concatenate(
        [heads_in[..., :x_dev], heads_in[..., bc_start:key_start]], axis=-1
    ).astype(jnp.float32)
    (scan_x, scan_b, scan_c, scan_step, scan_cum), prepare_pull = jax.vjp(
        mamba_prepare,
        mamba_in,
        step_heads.astype(jnp.float32),
        conv_rows,
        bias_rows,
        rate_rows,
        shift_rows,
    )
    scan_ins = (
        scan_x,
        scan_b,
        scan_c,
        scan_step,
        scan_cum,
        jnp.swapaxes(scan_step, 1, 2),
        jnp.swapaxes(scan_cum, 1, 2),
    )
    scan_y, scan_kept = scan_call(scan_forward_kernel, scan_ins, lambda j: j, False)
    skip_wide = jnp.repeat(skip_rows, HD)
    mamba_out = scan_y + skip_wide * scan_x
    positions = jnp.arange(full_len)
    queries = rotate(
        heads_in[..., x_dev:bc_start].astype(jnp.float32).reshape(
            seq_count, full_len, query_dev, HD
        ),
        positions,
        1.0,
    ).astype(jnp.bfloat16)
    key_rot = rotate(
        heads_in[..., key_start:value_start].astype(jnp.float32).reshape(
            seq_count, full_len, kv_dev, HD
        ),
        positions,
        1.0,
    ).astype(jnp.bfloat16)
    values = heads_in[..., value_start:send_cols].reshape(seq_count, full_len, kv_dev, HD)
    key_rot = jnp.repeat(key_rot, query_dev // kv_dev, axis=2)
    values = jnp.repeat(values, query_dev // kv_dev, axis=2)
    attn_out, logsum = attend_forward(queries, key_rot, values)
    back_send = jnp.concatenate(
        [
            mamba_out.astype(jnp.bfloat16),
            attn_out.reshape(seq_count, full_len, q_dev).astype(jnp.bfloat16),
        ],
        axis=-1,
    )
    back_send, out_full, gate_up_full, down_full = lax.optimization_barrier(
        (back_send, out_full, gate_up_full, down_full)
    )
    mamba_proj = out_full[:, :out_rows].reshape(mamba_width, -1)
    attn_proj = out_full[:, out_rows:].reshape(QH * HD, -1)
    back_tokens = exchange(to_parts(back_send))
    mamba_tok = join_heads(back_tokens[..., :x_dev])
    attn_tok = join_heads(back_tokens[..., x_dev:])
    sig_z = jax.nn.sigmoid(gate_z)
    silu_z = gate_z * sig_z
    gated_mixture = (mamba_tok.astype(jnp.float32) * silu_z).astype(jnp.bfloat16)
    branch_output = product("gle,ed->gld", gated_mixture, mamba_proj) + product(
        "gle,ed->gld", attn_tok, attn_proj
    )
    residual_stream = tokens_f + branch_output
    scale_two = rms_scale(residual_stream)
    second_normalized = (residual_stream * scale_two * gain_two.astype(jnp.float32)).astype(
        jnp.bfloat16
    )
    rows_all = lax.all_gather(second_normalized, "tp", axis=0, tiled=True)
    gate_up_values = product("gld,dcf->glcf", rows_all, gate_up_full)
    gate_part = gate_up_values[..., 0, :]
    up_part = gate_up_values[..., 1, :]
    sig_gate = jax.nn.sigmoid(gate_part)
    silu_gate = gate_part * sig_gate
    hidden_units = (silu_gate * up_part).astype(jnp.bfloat16)
    partial_out = product("glf,df->gld", hidden_units, down_full)
    mlp_out = lax.psum_scatter(
        partial_out.astype(jnp.bfloat16), "tp", scatter_dimension=0, tiled=True
    ).astype(jnp.float32)
    out_block = (residual_stream + mlp_out).astype(jnp.bfloat16)
    grad_hidden = product("gld,df->glf", cot_all, down_full)
    grad_down = product("gld,glf->df", cot_all, hidden_units)
    slope_gate = sig_gate * (1.0 + gate_part * (1.0 - sig_gate))
    grad_gate_up = jnp.stack(
        [grad_hidden * up_part * slope_gate, grad_hidden * silu_gate], axis=2
    ).astype(jnp.bfloat16)
    grad_gu_w = product("gld,glcf->dcf", rows_all, grad_gate_up)
    grad_rows_part = product("glcf,dcf->gld", grad_gate_up, gate_up_full)
    grad_normed_two = lax.psum_scatter(
        grad_rows_part.astype(jnp.bfloat16), "tp", scatter_dimension=0, tiled=True
    ).astype(jnp.float32)
    grad_residual, grad_gain_two = norm_back(
        residual_stream, scale_two, gain_two.astype(jnp.float32), grad_normed_two
    )
    grad_residual = grad_residual + cotangent.astype(jnp.float32)
    grad_branch = grad_residual.astype(jnp.bfloat16)
    grad_mamba_proj = product("gle,gld->ed", gated_mixture, grad_branch)
    grad_attn_proj = product("gle,gld->ed", attn_tok, grad_branch)
    grad_gated = product("gld,ed->gle", grad_branch, mamba_proj)
    slope_z = sig_z * (1.0 + gate_z * (1.0 - sig_z))
    grad_mamba_tok = (grad_gated * silu_z).astype(jnp.bfloat16)
    grad_z = grad_gated * mamba_tok.astype(jnp.float32) * slope_z
    grad_attn_tok = product("gld,ed->gle", grad_branch, attn_proj).astype(jnp.bfloat16)
    out_sums = scatter_sum(
        jnp.concatenate(
            [
                grad_mamba_proj.reshape(-1, out_rows, grad_mamba_proj.shape[1]),
                grad_attn_proj.reshape(
                    -1, attention_output_weight.shape[0], grad_attn_proj.shape[1]
                ),
            ],
            axis=1,
        ).astype(jnp.bfloat16),
        devices_axes,
    )
    gate_up_sum = scatter_sum(
        grad_gu_w.astype(jnp.bfloat16).reshape((-1,) + gate_up_weight.shape), ("fsdp", "ctx")
    )
    down_sum = scatter_sum(
        grad_down.astype(jnp.bfloat16).reshape((-1,) + down_weight.shape), ("fsdp", "ctx")
    )
    grad_heads = to_sequence(
        exchange(
            jnp.concatenate([to_heads(grad_mamba_tok), to_heads(grad_attn_tok)], axis=-1)
        )
    )
    grad_mamba = grad_heads[..., :x_dev].astype(jnp.float32)
    gx, gb, gc, gstep, gcum, gstep_row, gcum_row = scan_call(
        scan_backward_kernel,
        scan_ins + (scan_kept, grad_mamba),
        lambda j: full_len // SSD_BLK - 1 - j,
        True,
    )
    grad_skip = jnp.sum(
        (grad_mamba * scan_x).reshape(-1, heads_dev, HD), axis=(0, 2)
    )
    grad_pre, grad_step, grad_conv_w, grad_conv_b, grad_rate, grad_shift = prepare_pull(
        (
            gx + skip_wide * grad_mamba,
            gb,
            gc,
            gstep + jnp.swapaxes(gstep_row, 1, 2),
            gcum + jnp.swapaxes(gcum_row, 1, 2),
        )
    )
    grad_queries, grad_keys, grad_values = attend_backward(
        queries,
        key_rot,
        values,
        logsum,
        grad_heads[..., x_dev:].reshape(seq_count, full_len, query_dev, HD),
    )
    grad_queries = rotate(grad_queries, positions, -1.0)
    grad_keys = jnp.sum(
        grad_keys.reshape(seq_count, full_len, kv_dev, query_dev // kv_dev, HD), axis=3
    )
    grad_values = jnp.sum(
        grad_values.reshape(seq_count, full_len, kv_dev, query_dev // kv_dev, HD), axis=3
    )
    grad_keys = rotate(grad_keys, positions, -1.0)
    tokens_send = jnp.concatenate(
        [
            grad_pre[..., :x_dev],
            grad_queries.reshape(seq_count, full_len, q_dev),
            grad_pre[..., x_dev:],
            grad_keys.reshape(seq_count, full_len, kv_cols),
            grad_values.reshape(seq_count, full_len, kv_cols),
            grad_step,
            jnp.zeros((seq_count, full_len, step_cols - heads_dev), jnp.float32),
        ],
        axis=-1,
    ).astype(jnp.bfloat16)
    tokens_send, out_sums, gate_up_sum, down_sum, out_block = lax.optimization_barrier(
        (tokens_send, out_sums, gate_up_sum, down_sum, out_block)
    )
    tokens_back = exchange(to_parts(tokens_send))
    grad_x_conv = join_heads(tokens_back[..., :x_dev])
    grad_query_tok = join_heads(tokens_back[..., x_dev:bc_start])
    grad_bc = jnp.sum(tokens_back[..., bc_start:key_start].astype(jnp.float32), axis=0)

    def kv_sum(pieces):
        joined = join_heads(pieces).astype(jnp.float32)
        return jnp.sum(
            joined.reshape(seq_count, local_len, KVH, kv_copies, HD), axis=3
        ).reshape(seq_count, local_len, KVH * HD)

    grad_key_tok = kv_sum(tokens_back[..., key_start:value_start])
    grad_value_tok = kv_sum(tokens_back[..., value_start:send_cols])
    step_tok = join_heads(tokens_back[..., send_cols : send_cols + heads_dev])
    grad_zx = jnp.concatenate([grad_z.astype(jnp.bfloat16), grad_x_conv, grad_bc.astype(jnp.bfloat16)], axis=-1)
    grad_step_low = step_tok
    grad_qkv = jnp.concatenate(
        [
            grad_query_tok,
            grad_key_tok.astype(jnp.bfloat16),
            grad_value_tok.astype(jnp.bfloat16),
        ],
        axis=-1,
    )
    grad_normed_one = (
        product("gle,de->gld", grad_zx, zx_full)
        + product("gle,de->gld", grad_step_low, step_full)
        + product("gle,de->gld", grad_qkv, qkv_full)
    )
    grad_zx_w = product("gld,gle->de", first_normalized, grad_zx)
    grad_step_w = product("gld,gle->de", first_normalized, grad_step_low)
    grad_qkv_w = product("gld,gle->de", first_normalized, grad_qkv)
    grad_input, grad_gain_one = norm_back(
        tokens_f, scale_one, gain_one.astype(jnp.float32), grad_normed_one
    )
    grad_input = grad_input + grad_residual
    in_grads = (
        jnp.concatenate([grad_zx_w, grad_qkv_w, grad_step_w], axis=1)
        .astype(jnp.bfloat16)
        .reshape(-1, mixer_gain.shape[0], zx_cols + qkv_cols + MH)
    )
    middle = (zx_cols + qkv_cols) // 2
    in_sums = jnp.concatenate(
        [
            scatter_sum(in_grads[..., :middle], devices_axes),
            scatter_sum(in_grads[..., middle:], devices_axes, True),
        ],
        axis=-1,
    )
    conv_full = jnp.concatenate(
        [
            lax.dynamic_update_slice_in_dim(
                jnp.zeros((mamba_width, grad_conv_w.shape[1]), jnp.float32),
                grad_conv_w[:x_dev],
                ctx_index * x_dev,
                0,
            ),
            grad_conv_w[x_dev:],
        ],
        axis=0,
    )
    bias_full = jnp.concatenate(
        [
            lax.dynamic_update_slice_in_dim(
                jnp.zeros((mamba_width,), jnp.float32), grad_conv_b[:x_dev], ctx_index * x_dev, 0
            ),
            grad_conv_b[x_dev:],
        ],
        axis=0,
    )
    rate_full = lax.dynamic_update_slice_in_dim(
        jnp.zeros((MH,), jnp.float32), grad_rate, ctx_index * heads_dev, 0
    )
    shift_full = lax.dynamic_update_slice_in_dim(
        jnp.zeros((MH,), jnp.float32), grad_shift, ctx_index * heads_dev, 0
    )
    skip_full = lax.dynamic_update_slice_in_dim(
        jnp.zeros((MH,), jnp.float32), grad_skip, ctx_index * heads_dev, 0
    )
    flat_parts = [
        conv_full.T.reshape(-1),
        bias_full,
        rate_full,
        shift_full,
        skip_full,
        grad_gain_one,
        grad_gain_two,
    ]
    sizes = [part.shape[0] for part in flat_parts]
    total = sum(sizes)
    flat = jnp.concatenate(flat_parts + [jnp.zeros((-total % 1024,), jnp.float32)])
    flat = butterfly_sum(flat.reshape(-1, 128), devices_axes).reshape(-1)
    head_sums = []
    start = 0
    for size in sizes:
        head_sums.append(flat[start : start + size])
        start += size
    gain_rows = mixer_gain.shape[0]
    place = lax.axis_index(devices_axes) * gain_rows
    return (
        out_block,
        grad_input.astype(jnp.bfloat16),
        lax.dynamic_slice_in_dim(head_sums[5], place, gain_rows, 0),
        in_sums[:, :zx_cols],
        in_sums[:, zx_cols + qkv_cols :],
        in_sums[:, zx_cols : zx_cols + qkv_cols],
        head_sums[0].reshape(conv_full.shape[1], conv_full.shape[0]).T,
        head_sums[1],
        head_sums[2],
        head_sums[3],
        head_sums[4],
        out_sums[:out_rows],
        out_sums[out_rows:],
        lax.dynamic_slice_in_dim(head_sums[6], place, gain_rows, 0),
        gate_up_sum,
        down_sum,
    )


def solution(mesh):
    placed = (
        P(("fsdp", "tp"), "ctx", None),
        P(("fsdp", "tp"), "ctx", None),
        P(("fsdp", "ctx", "tp")),
        P(("fsdp", "ctx", "tp"), None),
        P(("fsdp", "ctx", "tp"), None),
        P(("fsdp", "ctx", "tp"), None),
        P(),
        P(),
        P(),
        P(),
        P(),
        P(("fsdp", "ctx", "tp"), None),
        P(("fsdp", "ctx", "tp"), None),
        P(("fsdp", "ctx", "tp")),
        P(("fsdp", "ctx"), None, "tp"),
        P(("fsdp", "ctx"), "tp"),
    )
    return jax.shard_map(
        on_device,
        mesh=mesh,
        in_specs=placed,
        out_specs=(
            P(("fsdp", "tp"), "ctx", None),
            P(("fsdp", "tp"), "ctx", None),
            P(("fsdp", "ctx", "tp")),
            P(("fsdp", "ctx", "tp"), None),
            P(("fsdp", "ctx", "tp"), None),
            P(("fsdp", "ctx", "tp"), None),
            P(),
            P(),
            P(),
            P(),
            P(),
            P(("fsdp", "ctx", "tp"), None),
            P(("fsdp", "ctx", "tp"), None),
            P(("fsdp", "ctx", "tp")),
            P(("fsdp", "ctx"), None, "tp"),
            P(("fsdp", "ctx"), "tp"),
        ),
        check_vma=False,
    )
```
